32 devices in a mesh: row: 4 (over x, core), col: 8 (over z, y).
Axes of the slice: x: 2, y: 2, z: 4, core: 2. Of those that a mesh axis runs over, the one named last changes fastest.
Arguments:
- blocks: bfloat16 [96, 16, 1024], P(('row', 'col')), may hold values from -1.5 to 1.5
- tile_ids: int32 [96, 8], P(('row', 'col')), may hold values from 0 to 127, all different within a row
- barrier: float32 [16384], P('row'), may hold values from 0.5 to 4
Outputs:
- panels: float32 [16384, 256], P('row')
- schur_rest: float32 [16384, 16384], P('row', 'col')
The draws below stay inside these ranges and needn't reach their ends.
Inputs may be any that keep to these rules, and one draw needn't show every extreme that they name: `tile_ids`: each commodity lists 8 different arc tiles, and every tile is listed by some commodity.
All inputs are finite; a program needn't handle non-finite values.
Results may differ from the reference program's by a relative error of at most 0.0015.
Values may be sent and summed in bfloat16 or wider, within the bound.
A program may use at most 128 MiB of HBM per device.

```python
import math
import jax
import jax.numpy as jnp
from jax import lax

TILE = 128
NT = 128
BT = 8
COLS = 16
PANEL = 128
PANELS = 2
COMM = 96
NA = 16384


def shard_levels(own_key, extent, split, low, largest):
    def one(axis_at, shards_of):
        steps = jax.random.uniform(jax.random.fold_in(jax.random.fold_in(own_key, 6), axis_at), (shards_of,), jnp.float32, low / len(split), largest / len(split))
        return jnp.repeat(jnp.exp(steps), extent[axis_at] // shards_of).reshape((-1,) + (1,) * (len(extent) - axis_at - 1))

    factor_of = one(*split[0])
    for cut in split[1:]:
        factor_of = factor_of * one(*cut)
    return factor_of


def picks_of(key, rows, number_of, top, lift):
    sequence = jax.random.permutation(jax.random.fold_in(key, 1), number_of)
    boost = sequence
    for power in range(3):
        boost = boost * boost // number_of
    boost = boost * lift // number_of
    tickets = jax.random.randint(jax.random.fold_in(key, 2), (rows, number_of), 0, 4096) + boost
    holders = jax.random.permutation(jax.random.fold_in(key, 3), rows)[jnp.arange(number_of) % rows]
    tickets = jnp.where(jnp.arange(rows)[:, None] == holders[None, :], 1 << 14, tickets)
    priority = tickets * number_of + jnp.arange(number_of)
    return lax.top_k(priority.astype(jnp.int32), top)[1].astype(jnp.int32)


def normal_values(key, extent, spread, limit, pieces=(), kind=jnp.bfloat16):
    level = shard_levels(key, extent, pieces, -0.22, 0.18) if pieces else 1.0
    entries = jax.random.normal(key, extent, jnp.float32) * spread * level
    return jnp.minimum(jnp.maximum(entries, -limit), limit).astype(kind)


def setup_inputs(seed: int = 0) -> dict:
    keys = jax.random.split(jax.random.key(seed), 4)
    return {
        "blocks": normal_values(keys[0], (COMM, COLS, BT * TILE), 0.25, 1.5, ((0, 32),)),
        "tile_ids": picks_of(keys[1], COMM, NT, BT, 1024),
        "barrier": jnp.clip(jnp.exp(math.log(4.0) - 2.0794415 * jax.random.uniform(keys[2], (NA,), jnp.float32) ** shard_levels(keys[2], (NA,), ((0, 4),), -0.2, 0.2)), 0.5, 4.0),
    }


def reference(blocks, tile_ids, barrier):
    schur_full = jnp.diag(barrier.astype(jnp.float32))
    offsets = jnp.arange(TILE, dtype=jnp.int32)

    def add_one(running, entry):
        block_now, tiles_now = entry
        gram_block = jnp.dot(block_now.T.astype(jnp.float32), block_now.astype(jnp.float32), preferred_element_type=jnp.float32)
        arc_index = (tiles_now[:, None] * TILE + offsets[None, :]).reshape(-1).astype(jnp.int32)
        return (running.at[arc_index[:, None], arc_index[None, :]].add(gram_block), None)
    schur_full, _ = lax.scan(add_one, schur_full, (blocks, tile_ids))
    arc_rows = jnp.arange(NA, dtype=jnp.int32)
    panel_list = []
    for panel_index in range(PANELS):
        low_edge = panel_index * PANEL
        high_edge = low_edge + PANEL
        factor = jnp.linalg.cholesky(schur_full[low_edge:high_edge, low_edge:high_edge])
        solved = jax.scipy.linalg.solve_triangular(factor, schur_full[:, low_edge:high_edge].T, lower=True).T
        placed = jnp.zeros((NA, PANEL), jnp.float32).at[low_edge:high_edge].set(factor)
        panel_now = jnp.where((arc_rows < low_edge)[:, None], 0.0, jnp.where((arc_rows < high_edge)[:, None], placed, solved))
        trailing = panel_now[high_edge:]
        update = jnp.dot(trailing, trailing.T, precision=lax.Precision.HIGHEST)
        schur_full = schur_full.at[high_edge:, high_edge:].add(-update)
        panel_list.append(panel_now)
    return (jnp.concatenate(panel_list, axis=1), schur_full)
```

```python
import functools

import jax
import jax.numpy as jnp
from jax import lax
from jax.experimental import pallas as pl
from jax.experimental.pallas import tpu as pltpu
from jax.sharding import PartitionSpec as P

TILE = 128
BT = 8
COLS = 16
PANEL = 128
PANELS = 2
WIDE = PANEL * PANELS
GROUP = 16
HIGH = lax.Precision.HIGHEST
MESH = pl.DeviceIdType.MESH


def gather_kernel(sizes, x_ref, s_ref, big_ref, small_ref, send_sem, recv_sem, own_sem):
    na, nb, nx, nc = sizes
    ncol = na * nb
    row_at, col_at = lax.axis_index("row"), lax.axis_index("col")
    a, b = col_at // nb, col_at % nb
    x, c = row_at // nc, row_at % nc

    def at(da, db, dx, dc):
        row = ((x + dx) % nx) * nc + (c + dc) % nc
        col = ((a + da) % na) * nb + (b + db) % nb
        return row, col

    def chunk(key):
        row, col = at(*key)
        return row * ncol + col

    def slot(key):
        return ((key[0] * nb + key[1]) * nx + key[2]) * nc + key[3]

    partners = [(d, 0, 0, 0) for d in range(1, na)]
    partners += [(0, d, 0, 0) for d in range(1, nb)]
    partners += [(0, 0, d, 0) for d in range(1, nx)]
    partners += [(0, 0, 0, d) for d in range(1, nc)]
    barrier = pltpu.get_barrier_semaphore()
    for p in partners:
        pl.semaphore_signal(barrier, inc=1, device_id=at(*p), device_id_type=MESH)
    pl.semaphore_wait(barrier, len(partners))

    own = (0, 0, 0, 0)
    keep = [
        pltpu.make_async_copy(x_ref, big_ref.at[chunk(own)], own_sem.at[0]),
        pltpu.make_async_copy(s_ref, small_ref.at[chunk(own)], own_sem.at[1]),
    ]
    started = []

    def send(key, axis):
        mine = chunk(key)
        for step in range(1, sizes[axis]):
            to = [0, 0, 0, 0]
            to[axis] = step
            there = list(key)
            there[axis] = (key[axis] - step) % sizes[axis]
            number = len(started)
            pairs = [
                (x_ref if key == own else big_ref.at[mine], big_ref.at[mine]),
                (s_ref if key == own else small_ref.at[mine], small_ref.at[mine]),
            ]
            for kind, (src, dst) in enumerate(pairs):
                copy = pltpu.make_async_remote_copy(
                    src_ref=src,
                    dst_ref=dst,
                    send_sem=send_sem.at[kind, number // 2],
                    recv_sem=recv_sem.at[kind, slot(there)],
                    device_id=at(*to),
                    device_id_type=MESH,
                )
                copy.start()
                started.append(copy)

    def arrive(key):
        mine = chunk(key)
        for kind, ref in enumerate((big_ref, small_ref)):
            pltpu.make_async_remote_copy(
                src_ref=ref.at[mine],
                dst_ref=ref.at[mine],
                send_sem=send_sem.at[kind, 0],
                recv_sem=recv_sem.at[kind, slot(key)],
                device_id=at(0, 0, 0, 1),
                device_id_type=MESH,
            ).wait_recv()

    send(own, 0)
    order = sorted(range(na), key=lambda d: min(d, na - d))
    first = {d: 1 if d % 2 == 0 else 2 for d in order}
    for d in order:
        key = (d, 0, 0, 0)
        if d:
            arrive(key)
        send(key, first[d])
        send(key, 3 - first[d])
        send(key, 3)
        if d == 0:
            for copy in keep:
                copy.start()
    for d in order:
        for step in range(1, sizes[first[d]]):
            key = [d, 0, 0, 0]
            key[first[d]] = step
            key = tuple(key)
            arrive(key)
            send(key, 3 - first[d])
            send(key, 3)
    for d in order:
        for step in range(1, sizes[3 - first[d]]):
            for before in range(sizes[first[d]]):
                key = [d, 0, 0, 0]
                key[first[d]] = before
                key[3 - first[d]] = step
                key = tuple(key)
                arrive(key)
                send(key, 3)
    for da in order:
        for db in range(nb):
            for dx in range(nx):
                arrive((da, db, dx, 1))
    for copy in started:
        copy.wait_send()
    for copy in keep:
        copy.wait()


def gather_all(x, small):
    nrow, ncol = lax.axis_size("row"), lax.axis_size("col")
    na = 4 if ncol % 4 == 0 else 1
    sizes = (na, ncol // na, nrow // 2, 2)
    count = nrow * ncol
    return pl.pallas_call(
        functools.partial(gather_kernel, sizes),
        out_shape=(
            jax.ShapeDtypeStruct((count,) + x.shape, x.dtype),
            jax.ShapeDtypeStruct((count,) + small.shape, small.dtype),
        ),
        in_specs=[pl.BlockSpec(memory_space=pl.ANY)] * 2,
        out_specs=(pl.BlockSpec(memory_space=pl.ANY),) * 2,
        scratch_shapes=[
            pltpu.SemaphoreType.DMA((2, count)),
            pltpu.SemaphoreType.DMA((2, count)),
            pltpu.SemaphoreType.DMA((2,)),
        ],
        compiler_params=pltpu.CompilerParams(collective_id=0, has_side_effects=True),
    )(x, small)


def assemble_kernel(
    comm, row_tiles, col_tiles, ids_ref, at_ref, blocks_ref, cols_ref, top_ref, edge_ref,
    bar_ref, rest_ref, panel_ref, left, right, lists, counts,
):
    step = pl.program_id(0)
    row_first, col_first = at_ref[0], at_ref[1]
    band = col_tiles * TILE

    @pl.when(step == 0)
    def _():
        left[...] = jnp.zeros_like(left)
        right[...] = jnp.zeros_like(right)

        def clear(i, _):
            counts[i] = 0
            return 0

        lax.fori_loop(0, row_tiles + 1, clear, 0)

        def enter(k, _):
            for s in range(BT):
                where = ids_ref[k * BT + s] - row_first
                inside = jnp.logical_and(where >= 0, where < row_tiles)
                where = jnp.where(inside, where, row_tiles)
                n = counts[where]
                lists[where * comm + jnp.minimum(n, comm - 1)] = k * BT + s
                counts[where] = n + 1
            return 0

        lax.fori_loop(0, comm, enter, 0)

    tile = row_first + step
    total = counts[step]

    def pick(chunk):
        base = chunk * GROUP
        some = jnp.minimum(total - base, GROUP)

        def one(j, _):
            entry = lists[step * comm + base + j]
            k, s = entry // BT, entry % BT
            src = pl.ds(pl.multiple_of(k * COLS, COLS), COLS)
            dst = pl.ds(pl.multiple_of(j * COLS, COLS), COLS)
            left[dst, :] = blocks_ref[src, pl.ds(pl.multiple_of(s * TILE, TILE), TILE)]
            right[dst, :] = cols_ref[src, :]
            return 0

        lax.fori_loop(0, some, one, 0)

        def blank(j, _):
            dst = pl.ds(pl.multiple_of(j * COLS, COLS), COLS)
            left[dst, :] = jnp.zeros((COLS, TILE), left.dtype)
            return 0

        lax.fori_loop(some, GROUP, blank, 0)

    def times():
        return lax.dot_general(
            left[...], right[...], (((0,), (0,)), ((), ())), preferred_element_type=jnp.float32
        )

    @pl.when(tile >= PANELS)
    def _():
        pick(0)
        got = times()
        rest_ref[...] = got[:, :band]
        panel_ref[...] = got[:, band : band + WIDE] + got[:, band + WIDE :]

        def more(chunk, _):
            pick(chunk)
            got = times()
            rest_ref[...] += got[:, :band]
            panel_ref[...] += got[:, band : band + WIDE] + got[:, band + WIDE :]
            return 0

        lax.fori_loop(1, (total + GROUP - 1) // GROUP, more, 0)

    @pl.when(tile < PANELS)
    def _():
        src = pl.ds(pl.multiple_of(jnp.minimum(tile, PANELS - 1) * TILE, TILE), TILE)
        rest_ref[...] = top_ref[src, :]
        panel_ref[...] = edge_ref[src, :]

    own = tile - col_first

    @pl.when(jnp.logical_and(own >= 0, own < col_tiles))
    def _():
        line = bar_ref[pl.ds(step, 1), :]
        there = lax.broadcasted_iota(jnp.int32, (TILE, TILE), 0)
        here = lax.broadcasted_iota(jnp.int32, (TILE, TILE), 1)
        spot = pl.ds(pl.multiple_of(own * TILE, TILE), TILE)
        rest_ref[:, spot] += jnp.where(there == here, jnp.broadcast_to(line, (TILE, TILE)), 0.0)


def assemble(ids, at, blocks, cols, top, edge, bar, row_tiles, col_tiles):
    comm = ids.shape[0] // BT
    band = col_tiles * TILE
    whole = pl.BlockSpec(memory_space=pltpu.VMEM)
    return pl.pallas_call(
        functools.partial(assemble_kernel, comm, row_tiles, col_tiles),
        grid_spec=pltpu.PrefetchScalarGridSpec(
            num_scalar_prefetch=2,
            grid=(row_tiles,),
            in_specs=[whole] * 5,
            out_specs=[
                pl.BlockSpec((TILE, band), lambda i, *_: (i, 0)),
                pl.BlockSpec((TILE, WIDE), lambda i, *_: (i, 0)),
            ],
            scratch_shapes=[
                pltpu.VMEM((GROUP * COLS, TILE), jnp.bfloat16),
                pltpu.VMEM((GROUP * COLS, cols.shape[1]), jnp.bfloat16),
                pltpu.SMEM(((row_tiles + 1) * comm,), jnp.int32),
                pltpu.SMEM((row_tiles + 1,), jnp.int32),
            ],
        ),
        out_shape=[
            jax.ShapeDtypeStruct((row_tiles * TILE, band), jnp.float32),
            jax.ShapeDtypeStruct((row_tiles * TILE, WIDE), jnp.float32),
        ],
        compiler_params=pltpu.CompilerParams(vmem_limit_bytes=48 * 1024 * 1024),
    )(ids, at, blocks, cols, top, edge, bar)


def expand(tiled, tile_list, first_tile, tile_count):
    wanted = first_tile + jnp.arange(tile_count, dtype=jnp.int32)
    onehot = (tile_list[:, :, None] == wanted[None, None, :]).astype(jnp.bfloat16)
    spread = jnp.einsum("kas,kjai->kjsi", onehot, tiled, preferred_element_type=jnp.float32)
    return spread.astype(jnp.bfloat16).reshape(
        tiled.shape[0] * tiled.shape[1], tile_count * tiled.shape[3]
    )


def mul(lhs, rhs, left, right, precision=HIGH):
    return lax.dot_general(
        lhs, rhs, (((left,), (right,)), ((), ())), precision=precision,
        preferred_element_type=jnp.float32,
    )


def split_two(v):
    hi = lax.reduce_precision(v, 8, 7)
    return hi.astype(jnp.bfloat16), (v - hi).astype(jnp.bfloat16)


def shards(blocks, tile_ids, barrier):
    nrow, ncol = lax.axis_size("row"), lax.axis_size("col")
    band_rows = barrier.shape[0]
    band_cols = band_rows * nrow // ncol
    row_tiles, col_tiles = band_rows // TILE, band_cols // TILE
    row_first = lax.axis_index("row") * row_tiles
    col_first = lax.axis_index("col") * col_tiles
    held = blocks.shape[0]
    depth = held * COLS
    spare = 8 * TILE - WIDE - held * BT
    small = jnp.concatenate(
        [barrier[:WIDE], tile_ids.reshape(-1).astype(jnp.float32), jnp.zeros((spare,), jnp.float32)]
    ).reshape(8, TILE)
    big, smalls = gather_all(blocks.reshape(depth, BT * TILE), small)
    smalls = smalls.reshape(smalls.shape[0], 8 * TILE)
    ids = smalls[:, WIDE : WIDE + held * BT].astype(jnp.int32).reshape(-1)
    top_bar = smalls[0, :WIDE]
    comm = ids.shape[0] // BT
    rows = big.reshape(comm * COLS, BT * TILE)
    tile_list = ids.reshape(comm, BT)
    tiled = rows.reshape(comm, COLS, BT, TILE)
    lead = expand(tiled, tile_list, 0, PANELS)
    cols = expand(tiled, tile_list, col_first, col_tiles)

    corner = mul(lead, lead, 0, 0, None) + jnp.diag(top_bar)
    eye = jnp.eye(PANEL, dtype=jnp.float32)
    f0 = jnp.linalg.cholesky(corner[:PANEL, :PANEL])
    w0 = jax.scipy.linalg.solve_triangular(f0, eye, lower=True)
    x10 = mul(corner[PANEL:, :PANEL], w0, 1, 1)
    f1 = jnp.linalg.cholesky(corner[PANEL:, PANEL:] - mul(x10, x10, 1, 1))
    w1 = jax.scipy.linalg.solve_triangular(f1, eye, lower=True)
    edge = jnp.concatenate(
        [
            jnp.concatenate([f0, jnp.zeros_like(f0)], axis=1),
            jnp.concatenate([x10, f1], axis=1),
        ],
        axis=0,
    )
    inv = jnp.concatenate(
        [
            jnp.concatenate([w0, jnp.zeros_like(w0)], axis=1),
            jnp.concatenate([-mul(mul(w1, x10, 1, 0), w0, 1, 0), w1], axis=1),
        ],
        axis=0,
    )
    i_hi, i_lo = split_two(inv)
    q = mul(lead, i_hi, 1, 1, None) + mul(lead, i_lo, 1, 1, None)
    q_hi, q_lo = split_two(q)
    t = mul(q_hi, cols, 0, 0, None) + mul(q_lo, cols, 0, 0, None)
    col_tile = col_first + jnp.arange(band_cols, dtype=jnp.int32)[None, :] // TILE
    done = jnp.arange(WIDE, dtype=jnp.int32)[:, None] // PANEL < col_tile
    t = jnp.where(done, t, 0.0)
    t_hi, t_lo = split_two(t)
    away = mul(q_hi, t_hi, 1, 0, None) + mul(q_hi, t_lo, 1, 0, None) + mul(q_lo, t_hi, 1, 0, None)
    rhs = jnp.concatenate(
        [(cols.astype(jnp.float32) - away).astype(jnp.bfloat16), q_hi, q_lo], axis=1
    )
    top = mul(lead, cols, 0, 0, None)
    lower = mul(x10, t[:PANEL], 1, 0)
    top = top - jnp.concatenate([jnp.zeros_like(lower), lower], axis=0)
    at = jnp.stack([row_first, col_first]).astype(jnp.int32)
    rest, panels = assemble(
        ids, at, rows, rhs, top, edge, barrier.reshape(row_tiles, TILE), row_tiles, col_tiles
    )
    return panels, rest


def solution(mesh):
    placed = (P(("row", "col"), None, None), P(("row", "col"), None), P("row"))
    return jax.shard_map(
        shards,
        mesh=mesh,
        in_specs=placed,
        out_specs=(P("row", None), P("row", "col")),
        check_vma=False,
    )
```

```python
import functools

import jax
import jax.numpy as jnp
from jax import lax
from jax.experimental import pallas as pl
from jax.experimental.pallas import tpu as pltpu
from jax.sharding import PartitionSpec as P

TILE = 128
BT = 8
COLS = 16
PANEL = 128
PANELS = 2
WIDE = PANEL * PANELS
GROUP = 16
HIGH = lax.Precision.HIGHEST
MESH = pl.DeviceIdType.MESH


def gather_kernel(sizes, x_ref, s_ref, big_ref, small_ref, send_sem, recv_sem, own_sem):
    na, nb, nx, nc = sizes
    ncol = na * nb
    row_at, col_at = lax.axis_index("row"), lax.axis_index("col")
    a, b = col_at // nb, col_at % nb
    x, c = row_at // nc, row_at % nc

    def at(da, db, dx, dc):
        row = ((x + dx) % nx) * nc + (c + dc) % nc
        col = ((a + da) % na) * nb + (b + db) % nb
        return row, col

    def chunk(key):
        row, col = at(*key)
        return row * ncol + col

    def slot(key):
        return ((key[0] * nb + key[1]) * nx + key[2]) * nc + key[3]

    partners = [(d, 0, 0, 0) for d in range(1, na)]
    partners += [(0, d, 0, 0) for d in range(1, nb)]
    partners += [(0, 0, d, 0) for d in range(1, nx)]
    partners += [(0, 0, 0, d) for d in range(1, nc)]
    barrier = pltpu.get_barrier_semaphore()
    for p in partners:
        pl.semaphore_signal(barrier, inc=1, device_id=at(*p), device_id_type=MESH)
    pl.semaphore_wait(barrier, len(partners))

    own = (0, 0, 0, 0)
    keep = [
        pltpu.make_async_copy(x_ref, big_ref.at[chunk(own)], own_sem.at[0]),
        pltpu.make_async_copy(s_ref, small_ref.at[chunk(own)], own_sem.at[1]),
    ]
    started = []

    def send(key, axis):
        mine = chunk(key)
        for step in range(1, sizes[axis]):
            to = [0, 0, 0, 0]
            to[axis] = step
            there = list(key)
            there[axis] = (key[axis] - step) % sizes[axis]
            number = len(started)
            pairs = [
                (x_ref if key == own else big_ref.at[mine], big_ref.at[mine]),
                (s_ref if key == own else small_ref.at[mine], small_ref.at[mine]),
            ]
            for kind, (src, dst) in enumerate(pairs):
                copy = pltpu.make_async_remote_copy(
                    src_ref=src,
                    dst_ref=dst,
                    send_sem=send_sem.at[kind, number // 2],
                    recv_sem=recv_sem.at[kind, slot(there)],
                    device_id=at(*to),
                    device_id_type=MESH,
                )
                copy.start()
                started.append(copy)

    def arrive(key):
        mine = chunk(key)
        for kind, ref in enumerate((big_ref, small_ref)):
            pltpu.make_async_remote_copy(
                src_ref=ref.at[mine],
                dst_ref=ref.at[mine],
                send_sem=send_sem.at[kind, 0],
                recv_sem=recv_sem.at[kind, slot(key)],
                device_id=at(0, 0, 0, 1),
                device_id_type=MESH,
            ).wait_recv()

    send(own, 0)
    order = sorted(range(na), key=lambda d: min(d, na - d))
    first = {d: 1 if d % 2 == 0 else 2 for d in order}
    for d in order:
        key = (d, 0, 0, 0)
        if d:
            arrive(key)
        send(key, first[d])
        send(key, 3 - first[d])
        send(key, 3)
        if d == 0:
            for copy in keep:
                copy.start()
    for d in order:
        for step in range(1, sizes[first[d]]):
            key = [d, 0, 0, 0]
            key[first[d]] = step
            key = tuple(key)
            arrive(key)
            send(key, 3 - first[d])
            send(key, 3)
    for d in order:
        for step in range(1, sizes[3 - first[d]]):
            for before in range(sizes[first[d]]):
                key = [d, 0, 0, 0]
                key[first[d]] = before
                key[3 - first[d]] = step
                key = tuple(key)
                arrive(key)
                send(key, 3)
    for da in order:
        for db in range(nb):
            for dx in range(nx):
                arrive((da, db, dx, 1))
    for copy in started:
        copy.wait_send()
    for copy in keep:
        copy.wait()


def gather_all(x, small):
    nrow, ncol = lax.axis_size("row"), lax.axis_size("col")
    na = 4 if ncol % 4 == 0 else 1
    sizes = (na, ncol // na, nrow // 2, 2)
    count = nrow * ncol
    return pl.pallas_call(
        functools.partial(gather_kernel, sizes),
        out_shape=(
            jax.ShapeDtypeStruct((count,) + x.shape, x.dtype),
            jax.ShapeDtypeStruct((count,) + small.shape, small.dtype),
        ),
        in_specs=[pl.BlockSpec(memory_space=pl.ANY)] * 2,
        out_specs=(pl.BlockSpec(memory_space=pl.ANY),) * 2,
        scratch_shapes=[
            pltpu.SemaphoreType.DMA((2, count)),
            pltpu.SemaphoreType.DMA((2, count)),
            pltpu.SemaphoreType.DMA((2,)),
        ],
        compiler_params=pltpu.CompilerParams(collective_id=0, has_side_effects=True),
    )(x, small)


def assemble_kernel(
    comm, row_tiles, col_tiles, ids_ref, at_ref, blocks_ref, cols_ref, q_ref, top_ref, edge_ref,
    bar_ref, rest_ref, panel_ref, left, right, lists, counts,
):
    step = pl.program_id(0)
    row_first, col_first = at_ref[0], at_ref[1]
    band = col_tiles * TILE

    @pl.when(step == 0)
    def _():
        left[...] = jnp.zeros_like(left)
        right[...] = jnp.zeros_like(right)

        def clear(i, _):
            counts[i] = 0
            return 0

        lax.fori_loop(0, row_tiles + 1, clear, 0)

        def enter(k, _):
            for s in range(BT):
                where = ids_ref[k * BT + s] - row_first
                inside = jnp.logical_and(where >= 0, where < row_tiles)
                where = jnp.where(inside, where, row_tiles)
                n = counts[where]
                lists[where * comm + jnp.minimum(n, comm - 1)] = k * BT + s
                counts[where] = n + 1
            return 0

        lax.fori_loop(0, comm, enter, 0)

    tile = row_first + step
    total = counts[step]

    def pick(chunk):
        base = chunk * GROUP
        some = jnp.minimum(total - base, GROUP)

        def one(j, _):
            entry = lists[step * comm + base + j]
            k, s = entry // BT, entry % BT
            src = pl.ds(pl.multiple_of(k * COLS, COLS), COLS)
            dst = pl.ds(pl.multiple_of(j * COLS, COLS), COLS)
            left[dst, :] = blocks_ref[src, pl.ds(pl.multiple_of(s * TILE, TILE), TILE)]
            right[dst, :band] = cols_ref[src, :]
            right[dst, band:] = q_ref[src, :]
            return 0

        lax.fori_loop(0, some, one, 0)

        def blank(j, _):
            dst = pl.ds(pl.multiple_of(j * COLS, COLS), COLS)
            left[dst, :] = jnp.zeros((COLS, TILE), left.dtype)
            return 0

        lax.fori_loop(some, GROUP, blank, 0)

    def times():
        return lax.dot_general(
            left[...], right[...], (((0,), (0,)), ((), ())), preferred_element_type=jnp.float32
        )

    @pl.when(tile >= PANELS)
    def _():
        pick(0)
        got = times()
        rest_ref[...] = got[:, :band]
        panel_ref[...] = got[:, band : band + WIDE] + got[:, band + WIDE :]

        def more(chunk, _):
            pick(chunk)
            got = times()
            rest_ref[...] += got[:, :band]
            panel_ref[...] += got[:, band : band + WIDE] + got[:, band + WIDE :]
            return 0

        lax.fori_loop(1, (total + GROUP - 1) // GROUP, more, 0)

    @pl.when(tile < PANELS)
    def _():
        src = pl.ds(pl.multiple_of(jnp.minimum(tile, PANELS - 1) * TILE, TILE), TILE)
        rest_ref[...] = top_ref[src, :]
        panel_ref[...] = edge_ref[src, :]

    own = tile - col_first

    @pl.when(jnp.logical_and(own >= 0, own < col_tiles))
    def _():
        line = bar_ref[pl.ds(step, 1), :]
        there = lax.broadcasted_iota(jnp.int32, (TILE, TILE), 0)
        here = lax.broadcasted_iota(jnp.int32, (TILE, TILE), 1)
        spot = pl.ds(pl.multiple_of(own * TILE, TILE), TILE)
        rest_ref[:, spot] += jnp.where(there == here, jnp.broadcast_to(line, (TILE, TILE)), 0.0)


def assemble(ids, at, blocks, cols, q, top, edge, bar, row_tiles, col_tiles):
    comm = ids.shape[0] // BT
    band = col_tiles * TILE
    whole = pl.BlockSpec(memory_space=pltpu.VMEM)
    return pl.pallas_call(
        functools.partial(assemble_kernel, comm, row_tiles, col_tiles),
        grid_spec=pltpu.PrefetchScalarGridSpec(
            num_scalar_prefetch=2,
            grid=(row_tiles,),
            in_specs=[whole] * 6,
            out_specs=[
                pl.BlockSpec((TILE, band), lambda i, *_: (i, 0)),
                pl.BlockSpec((TILE, WIDE), lambda i, *_: (i, 0)),
            ],
            scratch_shapes=[
                pltpu.VMEM((GROUP * COLS, TILE), jnp.bfloat16),
                pltpu.VMEM((GROUP * COLS, band + q.shape[1]), jnp.bfloat16),
                pltpu.SMEM(((row_tiles + 1) * comm,), jnp.int32),
                pltpu.SMEM((row_tiles + 1,), jnp.int32),
            ],
        ),
        out_shape=[
            jax.ShapeDtypeStruct((row_tiles * TILE, band), jnp.float32),
            jax.ShapeDtypeStruct((row_tiles * TILE, WIDE), jnp.float32),
        ],
        compiler_params=pltpu.CompilerParams(vmem_limit_bytes=48 * 1024 * 1024),
    )(ids, at, blocks, cols, q, top, edge, bar)


def factor_kernel(corner_ref, edge_ref, inv_ref, work):
    size = corner_ref.shape[0]
    work[:, :size] = corner_ref[...]
    there = lax.broadcasted_iota(jnp.int32, (size, size), 0)
    here = lax.broadcasted_iota(jnp.int32, (size, size), 1)
    work[:, size:] = jnp.where(there == here, 1.0, 0.0)
    sub = lax.broadcasted_iota(jnp.int32, (8, 1), 0)
    lane = lax.broadcasted_iota(jnp.int32, (8, TILE), 1)
    wide = lax.broadcasted_iota(jnp.int32, (8, size), 1)
    for first in range(0, size, 8):
        low = first // TILE * TILE
        high = low + TILE
        panel = work[first : first + 8, low : size + high]
        slab = panel[:, :TILE]
        line = [
            jnp.sum(jnp.where(lane == first - low + c, slab, 0.0), axis=1, keepdims=True)
            for c in range(8)
        ]
        for j in range(8):
            scale = lax.rsqrt(line[j][j : j + 1, :])
            drop = jnp.where(sub > j, line[j] * scale, 0.0)
            now = panel[j : j + 1, :] * scale
            panel = jnp.where(sub == j, now, panel - drop * now)
            for c in range(j + 1, 8):
                line[c] = line[c] - drop * (line[c][j : j + 1, :] * scale)
        upper = jnp.where(wide[:, low:] >= sub + first, panel[:, : size - low], 0.0)
        work[first : first + 8, low:size] = upper
        if low:
            work[first : first + 8, :low] = jnp.zeros((8, low), jnp.float32)
        inv_ref[first : first + 8, :high] = panel[:, size - low :]
        if high < size:
            inv_ref[first : first + 8, high:] = jnp.zeros((8, size - high), jnp.float32)
        after = first + 8
        if after < size:
            left = jnp.where(wide[:, low:] >= after, upper, 0.0)
            work[low:, low : size + high] -= lax.dot_general(
                left, panel, (((0,), (0,)), ((), ())), precision=HIGH,
                preferred_element_type=jnp.float32,
            )
    edge_ref[...] = work[:, :size].T


def factor(corner):
    spec = pl.BlockSpec(memory_space=pltpu.VMEM)
    size = corner.shape[0]
    return pl.pallas_call(
        factor_kernel,
        out_shape=[jax.ShapeDtypeStruct(corner.shape, jnp.float32)] * 2,
        in_specs=[spec],
        out_specs=[spec, spec],
        scratch_shapes=[pltpu.VMEM((size, 2 * size), jnp.float32)],
    )(corner)


def expand(tiled, tile_list, first_tile, tile_count):
    wanted = first_tile + jnp.arange(tile_count, dtype=jnp.int32)
    onehot = (tile_list[:, :, None] == wanted[None, None, :]).astype(jnp.bfloat16)
    spread = jnp.einsum("kas,kjai->kjsi", onehot, tiled, preferred_element_type=jnp.float32)
    return spread.astype(jnp.bfloat16).reshape(
        tiled.shape[0] * tiled.shape[1], tile_count * tiled.shape[3]
    )


def mul(lhs, rhs, left, right, precision=HIGH):
    return lax.dot_general(
        lhs, rhs, (((left,), (right,)), ((), ())), precision=precision,
        preferred_element_type=jnp.float32,
    )


def split_two(v):
    hi = lax.reduce_precision(v, 8, 7)
    return hi.astype(jnp.bfloat16), (v - hi).astype(jnp.bfloat16)


def shards(blocks, tile_ids, barrier):
    nrow, ncol = lax.axis_size("row"), lax.axis_size("col")
    band_rows = barrier.shape[0]
    band_cols = band_rows * nrow // ncol
    row_tiles, col_tiles = band_rows // TILE, band_cols // TILE
    row_first = lax.axis_index("row") * row_tiles
    col_first = lax.axis_index("col") * col_tiles
    held = blocks.shape[0]
    depth = held * COLS
    spare = 8 * TILE - WIDE - held * BT
    small = jnp.concatenate(
        [barrier[:WIDE], tile_ids.reshape(-1).astype(jnp.float32), jnp.zeros((spare,), jnp.float32)]
    ).reshape(8, TILE)
    big, smalls = gather_all(blocks.reshape(depth, BT * TILE), small)
    smalls = smalls.reshape(smalls.shape[0], 8 * TILE)
    ids = smalls[:, WIDE : WIDE + held * BT].astype(jnp.int32).reshape(-1)
    top_bar = smalls[0, :WIDE]
    comm = ids.shape[0] // BT
    rows = big.reshape(comm * COLS, BT * TILE)
    tile_list = ids.reshape(comm, BT)
    tiled = rows.reshape(comm, COLS, BT, TILE)
    lead = expand(tiled, tile_list, 0, PANELS)
    cols = expand(tiled, tile_list, col_first, col_tiles)

    corner = mul(lead, lead, 0, 0, None) + jnp.diag(top_bar)
    edge, inv = factor(corner)
    x10 = edge[PANEL:, :PANEL]
    i_hi, i_lo = split_two(inv)
    q = mul(lead, i_hi, 1, 1, None) + mul(lead, i_lo, 1, 1, None)
    q_hi, q_lo = split_two(q)
    t = mul(q_hi, cols, 0, 0, None)
    col_tile = col_first + jnp.arange(band_cols, dtype=jnp.int32)[None, :] // TILE
    done = jnp.arange(WIDE, dtype=jnp.int32)[:, None] // PANEL < col_tile
    t = jnp.where(done, t, 0.0)
    away = mul(q_hi, t.astype(jnp.bfloat16), 1, 0, None)
    rhs = (cols.astype(jnp.float32) - away).astype(jnp.bfloat16)
    qs = jnp.concatenate([q_hi, q_lo], axis=1)
    top = mul(lead, cols, 0, 0, None)
    lower = mul(x10, t[:PANEL], 1, 0)
    top = top - jnp.concatenate([jnp.zeros_like(lower), lower], axis=0)
    at = jnp.stack([row_first, col_first]).astype(jnp.int32)
    rest, panels = assemble(
        ids, at, rows, rhs, qs, top, edge, barrier.reshape(row_tiles, TILE), row_tiles, col_tiles
    )
    return panels, rest


def solution(mesh):
    placed = (P(("row", "col"), None, None), P(("row", "col"), None), P("row"))
    return jax.shard_map(
        shards,
        mesh=mesh,
        in_specs=placed,
        out_specs=(P("row", None), P("row", "col")),
        check_vma=False,
    )
```

```python
import functools

import jax
import jax.numpy as jnp
from jax import lax
from jax.experimental import pallas as pl
from jax.experimental.pallas import tpu as pltpu
from jax.sharding import PartitionSpec as P

TILE = 128
BT = 8
COLS = 16
PANEL = 128
PANELS = 2
WIDE = PANEL * PANELS
GROUP = 16
HIGH = lax.Precision.HIGHEST
MESH = pl.DeviceIdType.MESH


def gather_kernel(sizes, x_ref, s_ref, big_ref, small_ref, send_sem, recv_sem, own_sem):
    na, nb, nx, nc = sizes
    ncol = na * nb
    row_at, col_at = lax.axis_index("row"), lax.axis_index("col")
    a, b = col_at // nb, col_at % nb
    x, c = row_at // nc, row_at % nc

    def at(da, db, dx, dc):
        row = ((x + dx) % nx) * nc + (c + dc) % nc
        col = ((a + da) % na) * nb + (b + db) % nb
        return row, col

    def chunk(key):
        row, col = at(*key)
        return row * ncol + col

    def slot(key):
        return ((key[0] * nb + key[1]) * nx + key[2]) * nc + key[3]

    partners = [(d, 0, 0, 0) for d in range(1, na)]
    partners += [(0, d, 0, 0) for d in range(1, nb)]
    partners += [(0, 0, d, 0) for d in range(1, nx)]
    partners += [(0, 0, 0, d) for d in range(1, nc)]
    barrier = pltpu.get_barrier_semaphore()
    for p in partners:
        pl.semaphore_signal(barrier, inc=1, device_id=at(*p), device_id_type=MESH)
    pl.semaphore_wait(barrier, len(partners))

    own = (0, 0, 0, 0)
    keep = [
        pltpu.make_async_copy(x_ref, big_ref.at[chunk(own)], own_sem.at[0]),
        pltpu.make_async_copy(s_ref, small_ref.at[chunk(own)], own_sem.at[1]),
    ]
    started = []

    def send(key, axis):
        mine = chunk(key)
        for step in range(1, sizes[axis]):
            to = [0, 0, 0, 0]
            to[axis] = step
            there = list(key)
            there[axis] = (key[axis] - step) % sizes[axis]
            number = len(started)
            pairs = [
                (x_ref if key == own else big_ref.at[mine], big_ref.at[mine]),
                (s_ref if key == own else small_ref.at[mine], small_ref.at[mine]),
            ]
            for kind, (src, dst) in enumerate(pairs):
                copy = pltpu.make_async_remote_copy(
                    src_ref=src,
                    dst_ref=dst,
                    send_sem=send_sem.at[kind, number // 2],
                    recv_sem=recv_sem.at[kind, slot(there)],
                    device_id=at(*to),
                    device_id_type=MESH,
                )
                copy.start()
                started.append(copy)

    def arrive(key):
        mine = chunk(key)
        for kind, ref in enumerate((big_ref, small_ref)):
            pltpu.make_async_remote_copy(
                src_ref=ref.at[mine],
                dst_ref=ref.at[mine],
                send_sem=send_sem.at[kind, 0],
                recv_sem=recv_sem.at[kind, slot(key)],
                device_id=at(0, 0, 0, 1),
                device_id_type=MESH,
            ).wait_recv()

    send(own, 0)
    order = sorted(range(na), key=lambda d: min(d, na - d))
    first = {d: 1 if d % 2 == 0 else 2 for d in order}
    for d in order:
        key = (d, 0, 0, 0)
        if d:
            arrive(key)
        send(key, first[d])
        send(key, 3 - first[d])
        send(key, 3)
        if d == 0:
            for copy in keep:
                copy.start()
    for d in order:
        for step in range(1, sizes[first[d]]):
            key = [d, 0, 0, 0]
            key[first[d]] = step
            key = tuple(key)
            arrive(key)
            send(key, 3 - first[d])
            send(key, 3)
    for d in order:
        for step in range(1, sizes[3 - first[d]]):
            for before in range(sizes[first[d]]):
                key = [d, 0, 0, 0]
                key[first[d]] = before
                key[3 - first[d]] = step
                key = tuple(key)
                arrive(key)
                send(key, 3)
    for da in order:
        for db in range(nb):
            for dx in range(nx):
                arrive((da, db, dx, 1))
    for copy in started:
        copy.wait_send()
    for copy in keep:
        copy.wait()


def gather_all(x, small):
    nrow, ncol = lax.axis_size("row"), lax.axis_size("col")
    na = 4 if ncol % 4 == 0 else 1
    sizes = (na, ncol // na, nrow // 2, 2)
    count = nrow * ncol
    return pl.pallas_call(
        functools.partial(gather_kernel, sizes),
        out_shape=(
            jax.ShapeDtypeStruct((count,) + x.shape, x.dtype),
            jax.ShapeDtypeStruct((count,) + small.shape, small.dtype),
        ),
        in_specs=[pl.BlockSpec(memory_space=pl.ANY)] * 2,
        out_specs=(pl.BlockSpec(memory_space=pl.ANY),) * 2,
        scratch_shapes=[
            pltpu.SemaphoreType.DMA((2, count)),
            pltpu.SemaphoreType.DMA((2, count)),
            pltpu.SemaphoreType.DMA((2,)),
        ],
        compiler_params=pltpu.CompilerParams(collective_id=0, has_side_effects=True),
    )(x, small)


def assemble_kernel(
    comm, pairs, col_tiles, ids_ref, at_ref, blocks_ref, cols_ref, q_ref, top_ref, edge_ref,
    bar_ref, rest_ref, panel_ref, left, right, lists, counts,
):
    step = pl.program_id(0)
    row_first, col_first = at_ref[0], at_ref[1]
    band = col_tiles * TILE
    room = PANELS * comm

    @pl.when(step == 0)
    def _():
        left[...] = jnp.zeros_like(left)
        right[...] = jnp.zeros_like(right)

        def clear(i, _):
            counts[i] = 0
            return 0

        lax.fori_loop(0, pairs + 1, clear, 0)

        def enter(k, _):
            for s in range(BT):
                where = ids_ref[k * BT + s] - row_first
                inside = jnp.logical_and(where >= 0, where < pairs * PANELS)
                pair = jnp.where(inside, where >> 1, pairs)
                n = counts[pair]
                entry = (k * BT + s) * PANELS + (where & 1)
                lists[pair * room + jnp.minimum(n, room - 1)] = entry
                counts[pair] = n + 1
            return 0

        lax.fori_loop(0, comm, enter, 0)

    tile = row_first + step * PANELS
    total = counts[step]

    def pick(chunk):
        base = chunk * GROUP
        some = jnp.minimum(total - base, GROUP)

        def one(j, _):
            entry = lists[step * room + base + j]
            k, s, half = entry >> 4, (entry >> 1) & 7, entry & 1
            src = pl.ds(pl.multiple_of(k * COLS, COLS), COLS)
            dst = pl.ds(pl.multiple_of(j * COLS, COLS), COLS)
            block = blocks_ref[src, pl.ds(pl.multiple_of(s * TILE, TILE), TILE)]
            left[dst, pl.ds(pl.multiple_of(half * TILE, TILE), TILE)] = block
            left[dst, pl.ds(pl.multiple_of((1 - half) * TILE, TILE), TILE)] = jnp.zeros_like(block)
            right[dst, :band] = cols_ref[src, :]
            right[dst, band:] = q_ref[src, :]
            return 0

        lax.fori_loop(0, some, one, 0)

        def blank(j, _):
            dst = pl.ds(pl.multiple_of(j * COLS, COLS), COLS)
            left[dst, :] = jnp.zeros((COLS, WIDE), left.dtype)
            return 0

        lax.fori_loop(some, GROUP, blank, 0)

    def times(rows, at):
        return jnp.dot(rows, right[:, at : at + WIDE], preferred_element_type=jnp.float32)

    @pl.when(tile >= PANELS)
    def _():
        pick(0)
        rows = left[...].T
        for at in range(0, band, WIDE):
            rest_ref[:, at : at + WIDE] = times(rows, at)
        panel_ref[...] = times(rows, band) + times(rows, band + WIDE)

        def more(chunk, _):
            pick(chunk)
            rows = left[...].T
            for at in range(0, band, WIDE):
                rest_ref[:, at : at + WIDE] += times(rows, at)
            panel_ref[...] += times(rows, band) + times(rows, band + WIDE)
            return 0

        lax.fori_loop(1, (total + GROUP - 1) // GROUP, more, 0)

    @pl.when(tile < PANELS)
    def _():
        rest_ref[...] = top_ref[...]
        panel_ref[...] = edge_ref[...]

    own = tile - col_first

    @pl.when(jnp.logical_and(own >= 0, own < col_tiles))
    def _():
        line = bar_ref[pl.ds(step, 1), :]
        there = lax.broadcasted_iota(jnp.int32, (WIDE, WIDE), 0)
        here = lax.broadcasted_iota(jnp.int32, (WIDE, WIDE), 1)
        spot = pl.ds(pl.multiple_of(own * TILE, WIDE), WIDE)
        rest_ref[:, spot] += jnp.where(there == here, jnp.broadcast_to(line, (WIDE, WIDE)), 0.0)


def assemble(ids, at, blocks, cols, q, top, edge, bar, row_tiles, col_tiles):
    comm = ids.shape[0] // BT
    band = col_tiles * TILE
    pairs = row_tiles // PANELS
    whole = pl.BlockSpec(memory_space=pltpu.VMEM)
    return pl.pallas_call(
        functools.partial(assemble_kernel, comm, pairs, col_tiles),
        grid_spec=pltpu.PrefetchScalarGridSpec(
            num_scalar_prefetch=2,
            grid=(pairs,),
            in_specs=[whole] * 6,
            out_specs=[
                pl.BlockSpec((WIDE, band), lambda i, *_: (i, 0)),
                pl.BlockSpec((WIDE, WIDE), lambda i, *_: (i, 0)),
            ],
            scratch_shapes=[
                pltpu.VMEM((GROUP * COLS, WIDE), jnp.bfloat16),
                pltpu.VMEM((GROUP * COLS, band + q.shape[1]), jnp.bfloat16),
                pltpu.SMEM(((pairs + 1) * PANELS * comm,), jnp.int32),
                pltpu.SMEM((pairs + 1,), jnp.int32),
            ],
        ),
        out_shape=[
            jax.ShapeDtypeStruct((row_tiles * TILE, band), jnp.float32),
            jax.ShapeDtypeStruct((row_tiles * TILE, WIDE), jnp.float32),
        ],
        compiler_params=pltpu.CompilerParams(vmem_limit_bytes=48 * 1024 * 1024),
    )(ids, at, blocks, cols, q, top, edge, bar)


def factor_kernel(corner_ref, edge_ref, inv_ref, work):
    size = corner_ref.shape[0]
    work[:, :size] = corner_ref[...]
    there = lax.broadcasted_iota(jnp.int32, (size, size), 0)
    here = lax.broadcasted_iota(jnp.int32, (size, size), 1)
    work[:, size:] = jnp.where(there == here, 1.0, 0.0)
    sub = lax.broadcasted_iota(jnp.int32, (8, 1), 0)
    lane = lax.broadcasted_iota(jnp.int32, (8, TILE), 1)
    wide = lax.broadcasted_iota(jnp.int32, (8, size), 1)
    for first in range(0, size, 8):
        low = first // TILE * TILE
        high = low + TILE
        panel = work[first : first + 8, low : size + high]
        slab = panel[:, :TILE]
        line = [
            jnp.sum(jnp.where(lane == first - low + c, slab, 0.0), axis=1, keepdims=True)
            for c in range(8)
        ]
        for j in range(8):
            scale = lax.rsqrt(line[j][j : j + 1, :])
            drop = jnp.where(sub > j, line[j] * scale, 0.0)
            now = panel[j : j + 1, :] * scale
            panel = jnp.where(sub == j, now, panel - drop * now)
            for c in range(j + 1, 8):
                line[c] = line[c] - drop * (line[c][j : j + 1, :] * scale)
        upper = jnp.where(wide[:, low:] >= sub + first, panel[:, : size - low], 0.0)
        work[first : first + 8, low:size] = upper
        if low:
            work[first : first + 8, :low] = jnp.zeros((8, low), jnp.float32)
        inv_ref[first : first + 8, :high] = panel[:, size - low :]
        if high < size:
            inv_ref[first : first + 8, high:] = jnp.zeros((8, size - high), jnp.float32)
        after = first + 8
        if after < size:
            left = jnp.where(wide[:, low:] >= after, upper, 0.0)
            work[low:, low : size + high] -= lax.dot_general(
                left, panel, (((0,), (0,)), ((), ())), precision=HIGH,
                preferred_element_type=jnp.float32,
            )
    edge_ref[...] = work[:, :size].T


def factor(corner):
    spec = pl.BlockSpec(memory_space=pltpu.VMEM)
    size = corner.shape[0]
    return pl.pallas_call(
        factor_kernel,
        out_shape=[jax.ShapeDtypeStruct(corner.shape, jnp.float32)] * 2,
        in_specs=[spec],
        out_specs=[spec, spec],
        scratch_shapes=[pltpu.VMEM((size, 2 * size), jnp.float32)],
    )(corner)


def expand(tiled, tile_list, first_tile, tile_count):
    wanted = first_tile + jnp.arange(tile_count, dtype=jnp.int32)
    onehot = (tile_list[:, :, None] == wanted[None, None, :]).astype(jnp.bfloat16)
    spread = jnp.einsum("kas,kjai->kjsi", onehot, tiled, preferred_element_type=jnp.float32)
    return spread.astype(jnp.bfloat16).reshape(
        tiled.shape[0] * tiled.shape[1], tile_count * tiled.shape[3]
    )


def mul(lhs, rhs, left, right, precision=HIGH):
    return lax.dot_general(
        lhs, rhs, (((left,), (right,)), ((), ())), precision=precision,
        preferred_element_type=jnp.float32,
    )


def split_two(v):
    hi = lax.reduce_precision(v, 8, 7)
    return hi.astype(jnp.bfloat16), (v - hi).astype(jnp.bfloat16)


def shards(blocks, tile_ids, barrier):
    nrow, ncol = lax.axis_size("row"), lax.axis_size("col")
    band_rows = barrier.shape[0]
    band_cols = band_rows * nrow // ncol
    row_tiles, col_tiles = band_rows // TILE, band_cols // TILE
    row_first = lax.axis_index("row") * row_tiles
    col_first = lax.axis_index("col") * col_tiles
    held = blocks.shape[0]
    depth = held * COLS
    spare = 8 * TILE - WIDE - held * BT
    small = jnp.concatenate(
        [barrier[:WIDE], tile_ids.reshape(-1).astype(jnp.float32), jnp.zeros((spare,), jnp.float32)]
    ).reshape(8, TILE)
    big, smalls = gather_all(blocks.reshape(depth, BT * TILE), small)
    smalls = smalls.reshape(smalls.shape[0], 8 * TILE)
    ids = smalls[:, WIDE : WIDE + held * BT].astype(jnp.int32).reshape(-1)
    top_bar = smalls[0, :WIDE]
    comm = ids.shape[0] // BT
    rows = big.reshape(comm * COLS, BT * TILE)
    tile_list = ids.reshape(comm, BT)
    tiled = rows.reshape(comm, COLS, BT, TILE)
    lead = expand(tiled, tile_list, 0, PANELS)
    cols = expand(tiled, tile_list, col_first, col_tiles)

    corner = mul(lead, lead, 0, 0, None) + jnp.diag(top_bar)
    edge, inv = factor(corner)
    x10 = edge[PANEL:, :PANEL]
    i_hi, i_lo = split_two(inv)
    q = mul(lead, i_hi, 1, 1, None) + mul(lead, i_lo, 1, 1, None)
    q_hi, q_lo = split_two(q)
    t = mul(q_hi, cols, 0, 0, None)
    col_tile = col_first + jnp.arange(band_cols, dtype=jnp.int32)[None, :] // TILE
    done = jnp.arange(WIDE, dtype=jnp.int32)[:, None] // PANEL < col_tile
    t = jnp.where(done, t, 0.0)
    away = mul(q_hi, t.astype(jnp.bfloat16), 1, 0, None)
    rhs = (cols.astype(jnp.float32) - away).astype(jnp.bfloat16)
    qs = jnp.concatenate([q_hi, q_lo], axis=1)
    top = mul(lead, cols, 0, 0, None)
    lower = mul(x10, t[:PANEL], 1, 0)
    top = top - jnp.concatenate([jnp.zeros_like(lower), lower], axis=0)
    at = jnp.stack([row_first, col_first]).astype(jnp.int32)
    rest, panels = assemble(
        ids, at, rows, rhs, qs, top, edge, barrier.reshape(row_tiles // PANELS, WIDE), row_tiles, col_tiles
    )
    return panels, rest


def solution(mesh):
    placed = (P(("row", "col"), None, None), P(("row", "col"), None), P("row"))
    return jax.shard_map(
        shards,
        mesh=mesh,
        in_specs=placed,
        out_specs=(P("row", None), P("row", "col")),
        check_vma=False,
    )
```

```python
import functools

import jax
import jax.numpy as jnp
from jax import lax
from jax.experimental import pallas as pl
from jax.experimental.pallas import tpu as pltpu
from jax.sharding import PartitionSpec as P

TILE = 128
BT = 8
COLS = 16
PANEL = 128
PANELS = 2
WIDE = PANEL * PANELS
GROUP = 16
HIGH = lax.Precision.HIGHEST
MESH = pl.DeviceIdType.MESH


def gather_kernel(sizes, x_ref, s_ref, big_ref, small_ref, send_sem, recv_sem, own_sem):
    na, nb, nx, nc = sizes
    ncol = na * nb
    row_at, col_at = lax.axis_index("row"), lax.axis_index("col")
    a, b = col_at // nb, col_at % nb
    x, c = row_at // nc, row_at % nc

    def at(da, db, dx, dc):
        row = ((x + dx) % nx) * nc + (c + dc) % nc
        col = ((a + da) % na) * nb + (b + db) % nb
        return row, col

    def chunk(key):
        row, col = at(*key)
        return row * ncol + col

    def slot(key):
        return ((key[0] * nb + key[1]) * nx + key[2]) * nc + key[3]

    partners = [(d, 0, 0, 0) for d in range(1, na)]
    partners += [(0, d, 0, 0) for d in range(1, nb)]
    partners += [(0, 0, d, 0) for d in range(1, nx)]
    partners += [(0, 0, 0, d) for d in range(1, nc)]
    barrier = pltpu.get_barrier_semaphore()
    for p in partners:
        pl.semaphore_signal(barrier, inc=1, device_id=at(*p), device_id_type=MESH)
    pl.semaphore_wait(barrier, len(partners))

    own = (0, 0, 0, 0)
    keep = [
        pltpu.make_async_copy(x_ref, big_ref.at[chunk(own)], own_sem.at[0]),
        pltpu.make_async_copy(s_ref, small_ref.at[chunk(own)], own_sem.at[1]),
    ]
    started = []

    def send(key, axis):
        mine = chunk(key)
        for step in range(1, sizes[axis]):
            to = [0, 0, 0, 0]
            to[axis] = step
            there = list(key)
            there[axis] = (key[axis] - step) % sizes[axis]
            number = len(started)
            pairs = [
                (x_ref if key == own else big_ref.at[mine], big_ref.at[mine]),
                (s_ref if key == own else small_ref.at[mine], small_ref.at[mine]),
            ]
            for kind, (src, dst) in enumerate(pairs):
                copy = pltpu.make_async_remote_copy(
                    src_ref=src,
                    dst_ref=dst,
                    send_sem=send_sem.at[kind, number // 2],
                    recv_sem=recv_sem.at[kind, slot(there)],
                    device_id=at(*to),
                    device_id_type=MESH,
                )
                copy.start()
                started.append(copy)

    def arrive(key):
        mine = chunk(key)
        for kind, ref in enumerate((big_ref, small_ref)):
            pltpu.make_async_remote_copy(
                src_ref=ref.at[mine],
                dst_ref=ref.at[mine],
                send_sem=send_sem.at[kind, 0],
                recv_sem=recv_sem.at[kind, slot(key)],
                device_id=at(0, 0, 0, 1),
                device_id_type=MESH,
            ).wait_recv()

    send(own, 0)
    order = sorted(range(na), key=lambda d: min(d, na - d))
    first = {d: 1 if d % 2 == 0 else 2 for d in order}
    for d in order:
        key = (d, 0, 0, 0)
        if d:
            arrive(key)
        send(key, first[d])
        send(key, 3 - first[d])
        send(key, 3)
        if d == 0:
            for copy in keep:
                copy.start()
    for d in order:
        for step in range(1, sizes[first[d]]):
            key = [d, 0, 0, 0]
            key[first[d]] = step
            key = tuple(key)
            arrive(key)
            send(key, 3 - first[d])
            send(key, 3)
    for d in order:
        for step in range(1, sizes[3 - first[d]]):
            for before in range(sizes[first[d]]):
                key = [d, 0, 0, 0]
                key[first[d]] = before
                key[3 - first[d]] = step
                key = tuple(key)
                arrive(key)
                send(key, 3)
    for da in order:
        for db in range(nb):
            for dx in range(nx):
                arrive((da, db, dx, 1))
    for copy in started:
        copy.wait_send()
    for copy in keep:
        copy.wait()


def gather_all(x, small):
    nrow, ncol = lax.axis_size("row"), lax.axis_size("col")
    na = 4 if ncol % 4 == 0 else 1
    sizes = (na, ncol // na, nrow // 2, 2)
    count = nrow * ncol
    return pl.pallas_call(
        functools.partial(gather_kernel, sizes),
        out_shape=(
            jax.ShapeDtypeStruct((count,) + x.shape, x.dtype),
            jax.ShapeDtypeStruct((count,) + small.shape, small.dtype),
        ),
        in_specs=[pl.BlockSpec(memory_space=pl.ANY)] * 2,
        out_specs=(pl.BlockSpec(memory_space=pl.ANY),) * 2,
        scratch_shapes=[
            pltpu.SemaphoreType.DMA((2, count)),
            pltpu.SemaphoreType.DMA((2, count)),
            pltpu.SemaphoreType.DMA((2,)),
        ],
        compiler_params=pltpu.CompilerParams(collective_id=0, has_side_effects=True),
    )(x, small)


def assemble_kernel(
    comm, pairs, col_tiles, ids_ref, at_ref, blocks_ref, cols_ref, q_ref, top_ref, edge_ref,
    bar_ref, rest_ref, panel_ref, left, right, lists, counts,
):
    step = pl.program_id(0)
    row_first, col_first = at_ref[0], at_ref[1]
    band = col_tiles * TILE
    room = PANELS * comm

    @pl.when(step == 0)
    def _():
        left[...] = jnp.zeros_like(left)
        right[...] = jnp.zeros_like(right)

        def clear(i, _):
            counts[i] = 0
            return 0

        lax.fori_loop(0, pairs + 1, clear, 0)

        def enter(k, _):
            for s in range(BT):
                where = ids_ref[k * BT + s] - row_first
                inside = jnp.logical_and(where >= 0, where < pairs * PANELS)
                pair = jnp.where(inside, where >> 1, pairs)
                n = counts[pair]
                entry = (k * BT + s) * PANELS + (where & 1)
                lists[pair * room + jnp.minimum(n, room - 1)] = entry
                counts[pair] = n + 1
            return 0

        lax.fori_loop(0, comm, enter, 0, unroll=4)

    tile = row_first + step * PANELS
    total = counts[step]

    def pick(chunk):
        base = chunk * GROUP
        some = jnp.minimum(total - base, GROUP)

        def one(j, _):
            entry = lists[step * room + base + j]
            k, s, half = entry >> 4, (entry >> 1) & 7, entry & 1
            src = pl.ds(pl.multiple_of(k * COLS, COLS), COLS)
            dst = pl.ds(pl.multiple_of(j * COLS, COLS), COLS)
            block = blocks_ref[src, pl.ds(pl.multiple_of(s * TILE, TILE), TILE)]
            left[dst, pl.ds(pl.multiple_of(half * TILE, TILE), TILE)] = block
            left[dst, pl.ds(pl.multiple_of((1 - half) * TILE, TILE), TILE)] = jnp.zeros_like(block)
            right[dst, :band] = cols_ref[src, :]
            right[dst, band:] = q_ref[src, :]
            return 0

        lax.fori_loop(0, some, one, 0)

        def blank(j, _):
            dst = pl.ds(pl.multiple_of(j * COLS, COLS), COLS)
            left[dst, :] = jnp.zeros((COLS, WIDE), left.dtype)
            return 0

        lax.fori_loop(some, GROUP, blank, 0)

    def times(rows, at):
        return jnp.dot(rows, right[:, at : at + WIDE], preferred_element_type=jnp.float32)

    @pl.when(tile >= PANELS)
    def _():
        pick(0)
        rows = left[...].T
        for at in range(0, band, WIDE):
            rest_ref[:, at : at + WIDE] = times(rows, at)
        panel_ref[...] = times(rows, band) + times(rows, band + WIDE)

        def more(chunk, _):
            pick(chunk)
            rows = left[...].T
            for at in range(0, band, WIDE):
                rest_ref[:, at : at + WIDE] += times(rows, at)
            panel_ref[...] += times(rows, band) + times(rows, band + WIDE)
            return 0

        lax.fori_loop(1, (total + GROUP - 1) // GROUP, more, 0)

    @pl.when(tile < PANELS)
    def _():
        rest_ref[...] = top_ref[...]
        panel_ref[...] = edge_ref[...]

    own = tile - col_first

    @pl.when(jnp.logical_and(own >= 0, own < col_tiles))
    def _():
        line = bar_ref[pl.ds(step, 1), :]
        there = lax.broadcasted_iota(jnp.int32, (WIDE, WIDE), 0)
        here = lax.broadcasted_iota(jnp.int32, (WIDE, WIDE), 1)
        spot = pl.ds(pl.multiple_of(own * TILE, WIDE), WIDE)
        rest_ref[:, spot] += jnp.where(there == here, jnp.broadcast_to(line, (WIDE, WIDE)), 0.0)


def assemble(ids, at, blocks, cols, q, top, edge, bar, row_tiles, col_tiles):
    comm = ids.shape[0] // BT
    band = col_tiles * TILE
    pairs = row_tiles // PANELS
    whole = pl.BlockSpec(memory_space=pltpu.VMEM)
    return pl.pallas_call(
        functools.partial(assemble_kernel, comm, pairs, col_tiles),
        grid_spec=pltpu.PrefetchScalarGridSpec(
            num_scalar_prefetch=2,
            grid=(pairs,),
            in_specs=[whole] * 6,
            out_specs=[
                pl.BlockSpec((WIDE, band), lambda i, *_: (i, 0)),
                pl.BlockSpec((WIDE, WIDE), lambda i, *_: (i, 0)),
            ],
            scratch_shapes=[
                pltpu.VMEM((GROUP * COLS, WIDE), jnp.bfloat16),
                pltpu.VMEM((GROUP * COLS, band + q.shape[1]), jnp.bfloat16),
                pltpu.SMEM(((pairs + 1) * PANELS * comm,), jnp.int32),
                pltpu.SMEM((pairs + 1,), jnp.int32),
            ],
        ),
        out_shape=[
            jax.ShapeDtypeStruct((row_tiles * TILE, band), jnp.float32),
            jax.ShapeDtypeStruct((row_tiles * TILE, WIDE), jnp.float32),
        ],
        compiler_params=pltpu.CompilerParams(vmem_limit_bytes=48 * 1024 * 1024),
    )(ids, at, blocks, cols, q, top, edge, bar)


def factor_kernel(corner_ref, edge_ref, inv_ref, work):
    size = corner_ref.shape[0]
    work[:, :size] = corner_ref[...]
    there = lax.broadcasted_iota(jnp.int32, (size, size), 0)
    here = lax.broadcasted_iota(jnp.int32, (size, size), 1)
    work[:, size:] = jnp.where(there == here, 1.0, 0.0)
    sub = lax.broadcasted_iota(jnp.int32, (8, 1), 0)
    lane = lax.broadcasted_iota(jnp.int32, (8, TILE), 1)
    wide = lax.broadcasted_iota(jnp.int32, (8, size), 1)
    for first in range(0, size, 8):
        low = first // TILE * TILE
        high = low + TILE
        panel = work[first : first + 8, low : size + high]
        slab = panel[:, :TILE]
        line = [
            jnp.sum(jnp.where(lane == first - low + c, slab, 0.0), axis=1, keepdims=True)
            for c in range(8)
        ]
        for j in range(8):
            scale = lax.rsqrt(line[j][j : j + 1, :])
            drop = jnp.where(sub > j, line[j] * scale, 0.0)
            now = panel[j : j + 1, :] * scale
            panel = jnp.where(sub == j, now, panel - drop * now)
            for c in range(j + 1, 8):
                line[c] = line[c] - drop * (line[c][j : j + 1, :] * scale)
        upper = jnp.where(wide[:, low:] >= sub + first, panel[:, : size - low], 0.0)
        work[first : first + 8, low:size] = upper
        if low:
            work[first : first + 8, :low] = jnp.zeros((8, low), jnp.float32)
        inv_ref[first : first + 8, :high] = panel[:, size - low :]
        if high < size:
            inv_ref[first : first + 8, high:] = jnp.zeros((8, size - high), jnp.float32)
        after = first + 8
        if after < size:
            left = jnp.where(wide[:, low:] >= after, upper, 0.0)
            work[low:, low : size + high] -= lax.dot_general(
                left, panel, (((0,), (0,)), ((), ())), precision=HIGH,
                preferred_element_type=jnp.float32,
            )
    edge_ref[...] = work[:, :size].T


def factor(corner):
    spec = pl.BlockSpec(memory_space=pltpu.VMEM)
    size = corner.shape[0]
    return pl.pallas_call(
        factor_kernel,
        out_shape=[jax.ShapeDtypeStruct(corner.shape, jnp.float32)] * 2,
        in_specs=[spec],
        out_specs=[spec, spec],
        scratch_shapes=[pltpu.VMEM((size, 2 * size), jnp.float32)],
    )(corner)


def expand(tiled, tile_list, first_tile, tile_count):
    wanted = first_tile + jnp.arange(tile_count, dtype=jnp.int32)
    onehot = (tile_list[:, :, None] == wanted[None, None, :]).astype(jnp.bfloat16)
    spread = jnp.einsum("kas,kjai->kjsi", onehot, tiled, preferred_element_type=jnp.float32)
    return spread.astype(jnp.bfloat16).reshape(
        tiled.shape[0] * tiled.shape[1], tile_count * tiled.shape[3]
    )


def mul(lhs, rhs, left, right, precision=HIGH):
    return lax.dot_general(
        lhs, rhs, (((left,), (right,)), ((), ())), precision=precision,
        preferred_element_type=jnp.float32,
    )


def split_two(v):
    hi = lax.reduce_precision(v, 8, 7)
    return hi.astype(jnp.bfloat16), (v - hi).astype(jnp.bfloat16)


def shards(blocks, tile_ids, barrier):
    nrow, ncol = lax.axis_size("row"), lax.axis_size("col")
    band_rows = barrier.shape[0]
    band_cols = band_rows * nrow // ncol
    row_tiles, col_tiles = band_rows // TILE, band_cols // TILE
    row_first = lax.axis_index("row") * row_tiles
    col_first = lax.axis_index("col") * col_tiles
    held = blocks.shape[0]
    depth = held * COLS
    spare = 8 * TILE - WIDE - held * BT
    small = jnp.concatenate(
        [barrier[:WIDE], tile_ids.reshape(-1).astype(jnp.float32), jnp.zeros((spare,), jnp.float32)]
    ).reshape(8, TILE)
    big, smalls = gather_all(blocks.reshape(depth, BT * TILE), small)
    smalls = smalls.reshape(smalls.shape[0], 8 * TILE)
    ids = smalls[:, WIDE : WIDE + held * BT].astype(jnp.int32).reshape(-1)
    top_bar = smalls[0, :WIDE]
    comm = ids.shape[0] // BT
    rows = big.reshape(comm * COLS, BT * TILE)
    tile_list = ids.reshape(comm, BT)
    tiled = rows.reshape(comm, COLS, BT, TILE)
    lead = expand(tiled, tile_list, 0, PANELS)
    cols = expand(tiled, tile_list, col_first, col_tiles)

    corner = mul(lead, lead, 0, 0, None) + jnp.diag(top_bar)
    edge, inv = factor(corner)
    x10 = edge[PANEL:, :PANEL]
    i_hi, i_lo = split_two(inv)
    q = mul(lead, i_hi, 1, 1, None) + mul(lead, i_lo, 1, 1, None)
    q_hi, q_lo = split_two(q)
    t = mul(q_hi, cols, 0, 0, None)
    col_tile = col_first + jnp.arange(band_cols, dtype=jnp.int32)[None, :] // TILE
    done = jnp.arange(WIDE, dtype=jnp.int32)[:, None] // PANEL < col_tile
    t = jnp.where(done, t, 0.0)
    away = mul(q_hi, t.astype(jnp.bfloat16), 1, 0, None)
    rhs = (cols.astype(jnp.float32) - away).astype(jnp.bfloat16)
    qs = jnp.concatenate([q_hi, q_lo], axis=1)
    top = mul(lead, cols, 0, 0, None)
    lower = mul(x10, t[:PANEL], 1, 0)
    top = top - jnp.concatenate([jnp.zeros_like(lower), lower], axis=0)
    at = jnp.stack([row_first, col_first]).astype(jnp.int32)
    rest, panels = assemble(
        ids, at, rows, rhs, qs, top, edge, barrier.reshape(row_tiles // PANELS, WIDE), row_tiles, col_tiles
    )
    return panels, rest


def solution(mesh):
    placed = (P(("row", "col"), None, None), P(("row", "col"), None), P("row"))
    return jax.shard_map(
        shards,
        mesh=mesh,
        in_specs=placed,
        out_specs=(P("row", None), P("row", "col")),
        check_vma=False,
    )
```
